512 devices in a mesh: clu: 32 (over x, z), bank: 16 (over y, core).
Axes of the slice: x: 4, y: 8, z: 8, core: 2. Of those that a mesh axis runs over, the one named last changes fastest.
Arguments:
- queries: bfloat16 [131072, 3584], P(('clu', 'bank')), may hold values from -4 to 4
- bank: bfloat16 [32768, 3584], P(('clu', 'bank')), may hold values from -4 to 4
- cluster_ids: int32 [131072, 1], P(('clu', 'bank')), may hold values from 0 to 31; in each aligned block of 256 rows (0 to 255, 256 to 511, ...) at most 12 rows name the same one
- block_lists: int32 [131072, 8], P(('clu', 'bank')), may hold values from 0 to 15, all different within a row
- positive_ids: int32 [131072], P(('clu', 'bank')), may hold values from 0 to 1023
- loss_weights: float32 [131072], P(('clu', 'bank')), may hold values from 0.5 to 2
Outputs:
- query_grad: bfloat16 [131072, 3584], P(('clu', 'bank'))
- losses: bfloat16 [131072], P(('clu', 'bank'))
The draws below stay inside these ranges and needn't reach their ends.
Inputs may be any that keep to these rules, and one draw needn't show every extreme that they name: `cluster_ids`: at most 12 of the 256 queries of one device name the same cluster. `block_lists`: each query lists 8 different blocks.
All inputs are finite; a program needn't handle non-finite values.
Results may differ from the reference program's by a relative error of at most 0.0051.
Values may be sent and summed in bfloat16 or wider, within the bound.
A program may use at most 64 MiB of HBM per device.

```python
import math
import jax
import jax.numpy as jnp
import numpy as np
from jax import lax

D = 3584
QDEV = 256
BROWS = 64
CLUSTERS = 32
NBLK = 8
CAP = 12
GROUP = 1024
QUERIES = 131072
BANKROWS = 32768
N_CLU = 32
N_BANK = 16


def positions(key):
    spots = jax.random.randint(jax.random.fold_in(key, 101), (QUERIES,), 0, GROUP)
    return spots.at[0].set(GROUP - 1).astype(jnp.int32)


def draw_positive_ids(key, part):
    return positions(key)


def draw_bank(key, part):
    key = jax.random.fold_in(key, 7)
    return jax.random.truncated_normal(key, -4.0, 4.0, (BANKROWS, D), jnp.float32).astype(jnp.bfloat16)


def draw_queries(key, part):
    key = jax.random.fold_in(key, 11)
    return jax.random.truncated_normal(key, -4.0, 4.0, (QUERIES, D), jnp.float32).astype(jnp.bfloat16)


def shard_levels(key, dims, split, low, high):
    loudness = 1.0
    for axis_at, shards_of in split:
        steps = jax.random.uniform(jax.random.fold_in(jax.random.fold_in(key, 6), axis_at), (shards_of,), jnp.float32, low / len(split), high / len(split))
        loudness = loudness * jnp.repeat(jnp.exp(steps), dims[axis_at] // shards_of).reshape((-1,) + (1,) * (len(dims) - 1 - axis_at))
    return loudness


def distinct(rng, rows, count, top, lift):
    ranking = jax.random.permutation(jax.random.fold_in(rng, 1), count)
    pull = ranking
    for power in range(3):
        pull = pull * pull // count
    pull = pull * lift // count
    tickets = jax.random.randint(jax.random.fold_in(rng, 2), (rows, count), 0, 4096) + pull
    fixed_rows = jax.random.permutation(jax.random.fold_in(rng, 3), rows)[jnp.arange(count) % rows]
    tickets = jnp.where(jnp.arange(rows)[:, None] == fixed_rows[None, :], 1 << 14, tickets)
    score = tickets * count + jnp.arange(count)
    return lax.top_k(score.astype(jnp.int32), top)[1].astype(jnp.int32)


def deal_out(rng, own, number, rows, count, top, reach, slope):
    sequence = jax.random.permutation(rng, count)
    crowded, usual = load_shares(count, rows * top, reach, slope, True), load_shares(count, rows * top, reach, slope, False)
    places = jnp.arange(count)

    def named(lengths, turn):
        used = int((lengths > 0).sum())
        fixed = max(1, used // 4)
        shifted = fixed + (places - fixed + turn * (used - fixed)) % max(1, count - fixed)
        return jnp.zeros((count,), jnp.int32).at[sequence[jnp.where(places < fixed, places, shifted)]].set(jnp.asarray(lengths, jnp.int32))

    lengths = jnp.where(number % 4 == 0, named(crowded, number // 4), named(usual, number - number // 4 - 1))
    mixed = jax.random.permutation(jax.random.fold_in(own, 3), count)
    donor, sink = mixed[0:count // 2 * 2:2], mixed[1:count // 2 * 2:2]
    margin = jnp.minimum(lengths[donor] - 1, reach - lengths[sink]) // 2
    margin = jnp.where((donor == sequence[0]) | (sink == sequence[0]) | (lengths[sink] == 0), 0, jnp.maximum(margin, 0))
    shifted = jax.random.randint(jax.random.fold_in(own, 4), (count // 2,), 0, 1 << 20) % (margin + 1)
    lengths = lengths.at[donor].add(-shifted).at[sink].add(shifted)
    members = jnp.searchsorted(jnp.cumsum(lengths), jnp.arange(rows * top), side="right").astype(jnp.int32)
    table = members.reshape(top, rows).T
    table = table[jax.random.permutation(jax.random.fold_in(own, 1), rows)]
    turn = jax.random.randint(jax.random.fold_in(own, 2), (rows, 1), 0, top)
    return jnp.take_along_axis(table, (jnp.arange(top)[None, :] + turn) % top, axis=1)


def load_shares(amount, total, most, lean, full):
    weights = [(1 << 20) // math.isqrt(standing ** lean) + 1 for standing in range(1, amount + 1)]
    largest = most if full else min(most, max(-(-total // amount), total * weights[0] // sum(weights)))
    least = 1 if total - largest >= amount - 1 else 0
    given, rest = [largest] + [least] * (amount - 1), total - largest - least * (amount - 1)
    while rest > 0:
        movable = [i for i in range(1, amount) if given[i] < largest] or [i for i in range(1, amount) if given[i] < most]
        whole, left = sum([weights[i] for i in movable]), rest
        for i in movable:
            extra = min(most - given[i], max(1, left * weights[i] // whole), rest)
            given[i] = given[i] + extra
            rest = rest - extra
    return np.array(given)


def setup_inputs(seed: int = 0) -> dict:
    streams_of = jax.random.split(jax.random.key(seed), 7)
    queries = draw_queries(jax.random.fold_in(streams_of[6], 71), 0)
    bank = draw_bank(jax.random.fold_in(streams_of[6], 71), 0)
    cluster_ids_keys = jax.random.split(jax.random.fold_in(streams_of[2], 1), QUERIES // QDEV)
    cluster_ids_turns = jax.random.permutation(jax.random.fold_in(streams_of[2], 3), QUERIES // QDEV)
    cluster_ids = jax.vmap(lambda own, number: deal_out(jax.random.fold_in(streams_of[2], 2), own, number, QDEV, CLUSTERS, 1, CAP, 2))(cluster_ids_keys, cluster_ids_turns).reshape((QUERIES, 1))
    block_lists = distinct(streams_of[3], QUERIES, N_BANK, NBLK, 8192)
    positive_ids = draw_positive_ids(jax.random.fold_in(streams_of[6], 71), 0)
    loss_weights = jnp.clip(jnp.exp(math.log(2.0) - 1.3862944 * jax.random.uniform(streams_of[5], (QUERIES,), jnp.float32) ** shard_levels(streams_of[5], (QUERIES,), ((0, 512),), -0.2, 0.2)), 0.5, 2.0)
    return dict(queries=queries, bank=bank, cluster_ids=cluster_ids, block_lists=block_lists, positive_ids=positive_ids, loss_weights=loss_weights)


def reference(queries, bank, cluster_ids, block_lists, positive_ids, loss_weights):
    scale = 3.0 / math.sqrt(D)
    most = N_CLU * N_BANK * CAP
    clusters = cluster_ids[:, 0]
    block_ids = jnp.arange(N_BANK, dtype=jnp.int32)

    def one_cluster(cluster, carry):
        grads, losses = carry
        chosen = jnp.nonzero(clusters == cluster, size=most, fill_value=QUERIES)[0].astype(jnp.int32)
        rows = jnp.take(queries, chosen, axis=0, mode='clip')
        lists = jnp.take(block_lists, chosen, axis=0, mode='clip')
        positive = jnp.take(positive_ids, chosen, axis=0, mode='clip').astype(jnp.int32)
        weights = jnp.take(loss_weights, chosen, axis=0, mode='clip')
        keys = lax.dynamic_slice_in_dim(bank, (cluster * GROUP).astype(jnp.int32), GROUP, 0)
        logits = jnp.dot(rows, keys.T, preferred_element_type=jnp.float32) * scale
        block_mask = jnp.any(lists[:, :, None] == block_ids[None, None, :], axis=1)
        block_mask = block_mask | ((positive // BROWS)[:, None] == block_ids[None, :])
        allowed = jnp.repeat(block_mask, BROWS, axis=1).astype(jnp.int32)
        usable = allowed > 0
        top = lax.optimization_barrier(jnp.max(jnp.where(usable, logits, -jnp.inf), axis=1))
        total = lax.optimization_barrier(jnp.sum(jnp.where(usable, jnp.exp(logits - top[:, None]), 0.0), axis=1))
        lse = top + jnp.log(total)
        pos_logit = jnp.take_along_axis(logits, positive[:, None], axis=1)[:, 0]
        loss = (lse - pos_logit).astype(jnp.bfloat16)
        probs = jnp.where(usable, jnp.exp(logits - lse[:, None]), 0.0).astype(jnp.bfloat16)
        pulled = jnp.dot(probs, keys, preferred_element_type=jnp.float32)
        picked = jnp.take(keys, positive, axis=0).astype(jnp.float32)
        cached = (scale * (pulled - picked)).astype(jnp.bfloat16)
        grad = (weights[:, None] * cached.astype(jnp.float32)).astype(jnp.bfloat16)
        grads = grads.at[chosen].set(grad, mode='drop')
        losses = losses.at[chosen].set(loss, mode='drop')
        return (grads, losses)
    start = (jnp.zeros((QUERIES, D), jnp.bfloat16), jnp.zeros((QUERIES,), jnp.bfloat16))
    grads, losses = lax.fori_loop(0, CLUSTERS, one_cluster, start)
    return (grads, losses)
```

```python
import functools
import math

import jax
import jax.numpy as jnp
from jax import lax
from jax.experimental import pallas as pl
from jax.experimental.pallas import tpu as pltpu
from jax.sharding import PartitionSpec as P

MESH = pl.DeviceIdType.MESH
D = 3584
NX, NZ, NY = 4, 8, 8
NA, NB = 20, 12
PIECES = NA + NB
CAP = 12
ROWS = 16
PART = 896
MAIN = 3 * PART
WIDE = MAIN + 128
QDEV = 256
BROWS = 64
HALF = BROWS // 2
KEYS = 1024
KTILE = 256
BASE = (0, NA * ROWS)
COUNT = (NA * ROWS, NB * ROWS)
SCALE = 3.0 / math.sqrt(D)
BF = jnp.bfloat16
F32 = jnp.float32


def dot(a, b):
    return jnp.dot(a, b, preferred_element_type=F32)


def dot_t(a, b):
    return lax.dot_general(a, b, (((1,), (1,)), ((), ())), preferred_element_type=F32)


def iota(shape, dim):
    return lax.broadcasted_iota(jnp.int32, shape, dim)


def ones_where(cond):
    return jnp.where(cond, 1.0, 0.0).astype(BF)


def offsets(k, part):
    if part == 0:
        return k // 5, lax.rem(k % 5 + (NZ - 2), NZ)
    k = k - NA
    return k // 3, lax.rem(k % 3 + (NZ - 1), NZ)


def kernel(
    cid_ref,
    lists_ref,
    pos_ref,
    weight_ref,
    q_hbm,
    bank_hbm,
    grad_ref,
    loss_ref,
    q,
    keys,
    out,
    arrived,
    back,
    home,
    lastq,
    lg,
    wts,
    lastg,
    acc,
    local_sem,
    z_sem,
    go_send,
    go_recv,
    back_send,
    back_recv,
    ring_send,
    ring_recv,
    sib_send,
    sib_recv,
):
    clu, bank = lax.axis_index("clu"), lax.axis_index("bank")
    x, z = clu // NZ, clu % NZ
    y, core = bank // 2, bank % 2
    sibling = (clu, y * 2 + 1 - core)
    across = (x * NZ + lax.rem(z + 4, NZ), bank)

    def beside(d):
        return (clu, lax.rem(y + (1 if d == 0 else NY - 1), NY) * 2 + core)

    def at(dx, dz):
        return (lax.rem(x + dx, NX) * NZ + lax.rem(z + dz, NZ), bank)

    def remote(src, dst, send, recv, dev):
        return pltpu.make_async_remote_copy(
            src_ref=src, dst_ref=dst, send_sem=send, recv_sem=recv, device_id=dev, device_id_type=MESH
        )

    barrier = pltpu.get_barrier_semaphore()

    def greet(k, _):
        dx, dz = offsets(k, 0)

        @pl.when(k != 2)
        def _():
            pl.semaphore_signal(barrier, inc=1, device_id=at(dx, dz), device_id_type=MESH)

        return 0

    lax.fori_loop(0, NA, greet, 0)
    for dev in (sibling, across, beside(0), beside(1)):
        pl.semaphore_signal(barrier, inc=1, device_id=dev, device_id_type=MESH)

    own = pl.multiple_of((y * 2 + core) * BROWS, BROWS)
    get_q = pltpu.make_async_copy(q_hbm, q, local_sem.at[0])
    get_q.start()
    get_bank = pltpu.make_async_copy(bank_hbm, keys.at[0, pl.ds(own, BROWS)], local_sem.at[1])
    get_bank.start()

    eye = iota((QDEV, QDEV), 0) == iota((QDEV, QDEV), 1)

    def to_row(col):
        return jnp.sum(jnp.where(eye, col, 0.0), axis=0, keepdims=True)

    def to_col(row):
        return jnp.sum(jnp.where(eye, row, 0.0), axis=1, keepdims=True)

    cid = to_row(cid_ref[...].astype(F32)).astype(jnp.int32)
    dx = ((cid >> 3) - x + NX) & (NX - 1)
    dz = ((cid & 7) - z + NZ) & (NZ - 1)
    second = (dz >= 3) & (dz <= 5)
    piece = jnp.where(second, NA + dx * 3 + dz - 3, dx * 5 + ((dz + 2) & 7))
    named = iota((PIECES, QDEV), 0) == piece
    earlier = ones_where(iota((QDEV, QDEV), 0) < iota((QDEV, QDEV), 1))
    rank = jnp.sum(jnp.where(named, dot(ones_where(named), earlier), 0.0), axis=0, keepdims=True)
    rank = rank.astype(jnp.int32)
    slot = piece * ROWS + rank
    slot_last = piece * ROWS + CAP + (rank & 3)
    turn = rank >> 2
    slot_col = to_col(slot.astype(F32)).astype(jnp.int32)
    slot_last_col = to_col(slot_last.astype(F32)).astype(jnp.int32)
    turn_col = to_col(turn.astype(F32)).astype(jnp.int32)
    weight_col = to_col(weight_ref[...])
    pos_col = to_col(pos_ref[...].astype(F32)).astype(jnp.int32)
    lane = iota((QDEV, 128), 1)
    listed = lists_ref[:, 0:1] == lane
    for j in range(1, lists_ref.shape[1]):
        listed = listed | (lists_ref[:, j : j + 1] == lane)
    labels = jnp.where(listed & (lane < 16), 1.0, 0.0)
    labels = jnp.where(lane == 16, (pos_col >> 6).astype(F32), labels)
    labels = jnp.where(lane == 17, (pos_col & 63).astype(F32), labels).astype(BF)

    pl.semaphore_wait(barrier, NA - 1 + 4)

    z_copy = remote(bank_hbm, keys.at[1, pl.ds(own, BROWS)], z_sem.at[0], z_sem.at[1], across)
    z_copy.start()

    def rows_of(part, d, s, h):
        src = lax.rem(y + (NY - s if d == 0 else s), NY) * 2 + core
        return keys.at[part, pl.ds(pl.multiple_of(src * BROWS + h * HALF, HALF), HALF)]

    def ring(part, d, s, h):
        ref = rows_of(part, d, s - 1, h)
        src = bank_hbm.at[pl.ds(h * HALF, HALF)] if part == 0 and s == 1 else ref
        return remote(src, ref, ring_send.at[part, d, s - 1, h], ring_recv.at[part, d, s - 1, h], beside(d))

    def to_sibling(part, d, s, h):
        ref = rows_of(part, d, s, h)
        src = bank_hbm.at[pl.ds(h * HALF, HALF)] if part == 0 and s == 0 else ref
        return remote(src, ref, sib_send.at[part, d, s, h], sib_recv.at[part, d, s, h], sibling)

    def halves(s, d):
        return (0, 1) if s < 4 else (d,)

    def ring_begin(part):
        for h in (0, 1):
            for d in (0, 1):
                ring(part, d, 1, h).start()
        for h in (0, 1):
            to_sibling(part, 0, 0, h).start()

    def ring_step(part, s, h):
        for d in (0, 1):
            if h in halves(s, d):
                ring(part, d, s, h).wait_recv()
                if s < 4 and h in halves(s + 1, d):
                    ring(part, d, s + 1, h).start()
                to_sibling(part, d, s, h).start()

    def ring_end(part):
        for h in (0, 1):
            to_sibling(part, 0, 0, h).wait()
        for s in range(1, 5):
            for d in (0, 1):
                for h in halves(s, d):
                    ring(part, d, s, h).wait_send()
                    to_sibling(part, d, s, h).wait()

    ring_begin(0)

    def piece_rows(ref, k):
        return ref.at[pl.ds(pl.multiple_of(k * ROWS, ROWS), ROWS)]

    def go(k, part):
        dx, dz = offsets(k, part)
        return remote(piece_rows(out, k), piece_rows(arrived, k), go_send.at[k], go_recv.at[k], at(dx, dz))

    def come(k, part):
        dx, dz = offsets(k, part)
        dev = at(lax.rem(NX - dx, NX), lax.rem(NZ - dz, NZ))
        return remote(piece_rows(back, k), piece_rows(home, k), back_send.at[k], back_recv.at[k], dev)

    SELF = (2, NA + 1)
    stay_go = [
        pltpu.make_async_copy(piece_rows(out, SELF[p]), piece_rows(arrived, SELF[p]), local_sem.at[2 + p])
        for p in (0, 1)
    ]
    stay_come = [
        pltpu.make_async_copy(piece_rows(back, SELF[p]), piece_rows(home, SELF[p]), local_sem.at[4 + p])
        for p in (0, 1)
    ]

    def each(lo, hi, part, act):
        def step(k, _):
            @pl.when(k != SELF[part])
            def _():
                act(k)

            return 0

        lax.fori_loop(lo, hi, step, 0)

    get_q.wait()

    def pack(base, count):
        row = base + iota((count, QDEV), 0)
        main = ones_where(row == slot)
        out[base : base + count, MAIN:WIDE] = dot(main, labels).astype(BF)

        def step(t, _):
            cols = pl.ds(pl.multiple_of(t * PART, 128), PART)
            last = ones_where((row == slot_last) & (turn == t))
            out[base : base + count, cols] = (dot(main, q[:, cols]) + dot(last, q[:, MAIN:D])).astype(BF)
            return 0

        lax.fori_loop(0, 3, step, 0)

    for base, count in ((0, 160), (160, 160)):
        pack(base, count)
        each(base // ROWS, (base + count) // ROWS, 0, lambda k: go(k, 0).start())
    stay_go[0].start()
    pack(BASE[1], COUNT[1])
    each(NA, PIECES, 1, lambda k: go(k, 1).start())
    stay_go[1].start()

    def gather_last(part):
        base, count = BASE[part], COUNT[part]
        i, j = iota((count, count), 0), iota((count, count), 1)
        total = None
        for t in range(3):
            pick = ones_where((i >> 4 == j >> 4) & ((i & 15) == (j & 15) - CAP + 4 * t) & ((j & 15) >= CAP))
            term = dot(pick, arrived[base : base + count, t * PART : (t + 1) * PART])
            total = term if total is None else total + term
        lastq[base : base + count, :] = total.astype(BF)

    def logits(part):
        base, count = BASE[part], COUNT[part]

        def step(j, _):
            rows = pl.ds(pl.multiple_of(j * KTILE, KTILE), KTILE)
            total = dot_t(arrived[base : base + count, 0:MAIN], keys[part, rows, 0:MAIN])
            total = total + dot_t(lastq[base : base + count, :], keys[part, rows, MAIN:D])
            lg[base : base + count, rows] = total * SCALE
            return 0

        lax.fori_loop(0, KEYS // KTILE, step, 0)

    def softmax(part):
        base, count = BASE[part], COUNT[part]
        sub = 64
        kblock = iota((128, KEYS), 1) >> 6
        spread = ones_where(kblock == iota((128, KEYS), 0))

        def step(i, _):
            rows = pl.ds(pl.multiple_of(base + i * sub, sub), sub)
            tags = arrived[rows, MAIN:WIDE]
            l = lg[rows, :]
            high = tags[:, 16:17].astype(F32)
            pos = (high * 64.0 + tags[:, 17:18].astype(F32)).astype(jnp.int32)
            key = iota((sub, KEYS), 1)
            allowed = (dot(tags, spread) > 0.5) | (key >> 6 == high.astype(jnp.int32))
            hot = key == pos
            usable = jnp.where(allowed, l, -1e30)
            top = jnp.max(usable, axis=1, keepdims=True)
            e = jnp.exp(usable - top)
            total = jnp.sum(e, axis=1, keepdims=True)
            lse = top + jnp.log(total)
            loss = lse - jnp.sum(jnp.where(hot, l, 0.0), axis=1, keepdims=True)
            probs = (e * (1.0 / total)).astype(BF).astype(F32)
            wts[rows, :] = jnp.where(hot, probs - 1.0, probs).astype(BF)
            back[rows, MAIN:WIDE] = jnp.where(iota((sub, 128), 1) == 0, loss, 0.0).astype(BF)
            return 0

        lax.fori_loop(0, count // sub, step, 0)

    def pull(part):
        base, count = BASE[part], COUNT[part]
        lastg[0:count, :] = (dot(wts[base : base + count, :], keys[part, :, MAIN:D]) * SCALE).astype(BF)
        i, j = iota((count, count), 0), iota((count, count), 1)
        upper = iota((count, PART), 0) & 15

        def step(t, _):
            cols = pl.ds(pl.multiple_of(t * PART, 128), PART)
            main = dot(wts[base : base + count, :], keys[part, :, cols]) * SCALE
            put = ones_where((i >> 4 == j >> 4) & ((i & 15) >= CAP) & ((j & 15) == (i & 15) - CAP + 4 * t))
            low = dot(put, lastg[0:count, :])
            back[base : base + count, cols] = jnp.where(upper < CAP, main, low).astype(BF)
            return 0

        lax.fori_loop(0, 3, step, 0)

    def unpack(part):
        base, count = BASE[part], COUNT[part]
        col = base + iota((QDEV, count), 1)
        main = ones_where(slot_col == col)

        def step(t, _):
            cols = pl.ds(pl.multiple_of(t * PART, 128), PART)
            last = ones_where((slot_last_col == col) & (turn_col == t))
            block = home[base : base + count, cols]
            if part == 0:
                acc[:, cols] = dot(main, block)
            else:
                grad_ref[:, cols] = ((acc[:, cols] + dot(main, block)) * weight_col).astype(BF)
            tail = dot(last, block)
            acc[:, MAIN:D] = tail if part == 0 else acc[:, MAIN:D] + tail
            return 0

        if part == 0:
            col0 = iota((QDEV, count), 1)
            total = None
            for t in range(3):
                cols = slice(t * PART, (t + 1) * PART)
                last = ones_where((slot_last_col == col0) & (turn_col == t))
                acc[:, cols] = dot(main, home[base : base + count, cols])
                term = dot(last, home[base : base + count, cols])
                total = term if total is None else total + term
            acc[:, MAIN:D] = total
        else:
            lax.fori_loop(0, 3, step, 0)
            grad_ref[:, MAIN:D] = (acc[:, MAIN:D] * weight_col).astype(BF)
        return dot(main, home[base : base + count, MAIN:WIDE])

    for s, h in ((1, 0), (1, 1), (2, 0), (2, 1), (3, 0), (3, 1)):
        ring_step(0, s, h)
    z_copy.wait_recv()
    ring_begin(1)
    ring_step(0, 4, 0)
    ring_step(0, 4, 1)
    ring_end(0)
    get_bank.wait()

    ring_step(1, 1, 0)
    each(0, NA, 0, lambda k: go(k, 0).wait_recv())
    stay_go[0].wait()
    gather_last(0)
    logits(0)
    ring_step(1, 1, 1)
    softmax(0)
    ring_step(1, 2, 0)
    pull(0)
    each(0, NA, 0, lambda k: come(k, 0).start())
    stay_come[0].start()
    ring_step(1, 2, 1)
    each(NA, PIECES, 1, lambda k: go(k, 1).wait_recv())
    stay_go[1].wait()
    gather_last(1)
    for s, h in ((3, 0), (3, 1), (4, 0), (4, 1)):
        ring_step(1, s, h)
    ring_end(1)

    logits(1)
    softmax(1)
    pull(1)
    each(NA, PIECES, 1, lambda k: come(k, 1).start())
    stay_come[1].start()

    each(0, NA, 0, lambda k: come(k, 0).wait_recv())
    stay_come[0].wait()
    losses = unpack(0)
    z_copy.wait_send()
    each(0, NA, 0, lambda k: go(k, 0).wait_send())
    each(NA, PIECES, 1, lambda k: go(k, 1).wait_send())
    each(0, NA, 0, lambda k: come(k, 0).wait_send())
    each(NA, PIECES, 1, lambda k: come(k, 1).wait_recv())
    stay_come[1].wait()
    losses = losses + unpack(1)
    loss_ref[...] = to_row(losses[:, 0:1])
    each(NA, PIECES, 1, lambda k: come(k, 1).wait_send())


def body(queries, bank, cluster_ids, block_lists, positive_ids, loss_weights):
    vmem = pl.BlockSpec(memory_space=pltpu.VMEM)
    hbm = pl.BlockSpec(memory_space=pl.ANY)
    dma = pltpu.SemaphoreType.DMA
    slots = (PIECES * ROWS, WIDE)
    grad, loss = pl.pallas_call(
        kernel,
        out_shape=(
            jax.ShapeDtypeStruct((QDEV, D), BF),
            jax.ShapeDtypeStruct((1, QDEV), F32),
        ),
        in_specs=[vmem, vmem, vmem, vmem, hbm, hbm],
        out_specs=(vmem, vmem),
        scratch_shapes=[
            pltpu.VMEM((QDEV, D), BF),
            pltpu.VMEM((2, KEYS, D), BF),
            pltpu.VMEM(slots, BF),
            pltpu.VMEM(slots, BF),
            pltpu.VMEM(slots, BF),
            pltpu.VMEM(slots, BF),
            pltpu.VMEM((PIECES * ROWS, PART), BF),
            pltpu.VMEM((PIECES * ROWS, KEYS), F32),
            pltpu.VMEM((PIECES * ROWS, KEYS), BF),
            pltpu.VMEM((COUNT[0], PART), BF),
            pltpu.VMEM((QDEV, D), F32),
            dma((6,)),
            dma((2,)),
            dma((PIECES,)),
            dma((PIECES,)),
            dma((PIECES,)),
            dma((PIECES,)),
            dma((2, 2, 4, 2)),
            dma((2, 2, 4, 2)),
            dma((2, 2, 5, 2)),
            dma((2, 2, 5, 2)),
        ],
        compiler_params=pltpu.CompilerParams(
            collective_id=0, has_side_effects=True, vmem_limit_bytes=60 * 1024 * 1024
        ),
        cost_estimate=pl.CostEstimate(flops=10**10, bytes_accessed=10**7, transcendentals=10**6),
    )(
        cluster_ids,
        block_lists,
        positive_ids.reshape(1, QDEV),
        loss_weights.reshape(1, QDEV),
        queries,
        bank,
    )
    return grad, loss.reshape(QDEV).astype(BF)


def solution(mesh):
    rows = P(("clu", "bank"), None)
    flat = P(("clu", "bank"))
    return jax.shard_map(
        body,
        mesh=mesh,
        in_specs=(rows, rows, rows, rows, flat, flat),
        out_specs=(rows, flat),
        check_vma=False,
    )
```

```python
import functools
import math

import jax
import jax.numpy as jnp
from jax import lax
from jax.experimental import pallas as pl
from jax.experimental.pallas import tpu as pltpu
from jax.sharding import PartitionSpec as P

MESH = pl.DeviceIdType.MESH
D = 3584
NX, NZ, NY = 4, 8, 8
NA, NB = 20, 12
PIECES = NA + NB
CAP = 12
ROWS = 16
PART = 896
MAIN = 3 * PART
WIDE = MAIN + 128
QDEV = 256
BROWS = 64
HALF = BROWS // 2
KEYS = 1024
KTILE = 256
BASE = (0, NA * ROWS)
COUNT = (NA * ROWS, NB * ROWS)
SCALE = 3.0 / math.sqrt(D)
BF = jnp.bfloat16
F32 = jnp.float32


def dot(a, b):
    return jnp.dot(a, b, preferred_element_type=F32)


def dot_t(a, b):
    return lax.dot_general(a, b, (((1,), (1,)), ((), ())), preferred_element_type=F32)


def iota(shape, dim):
    return lax.broadcasted_iota(jnp.int32, shape, dim)


def ones_where(cond):
    return jnp.where(cond, 1.0, 0.0).astype(BF)


def offsets(k, part):
    k = k - part * NA
    turn, dx = k // NX, k % NX
    odd = turn % 2
    return dx, odd * ((turn + 1) // 2) + (1 - odd) * lax.rem(NZ - turn // 2, NZ)


def kernel(
    cid_ref,
    lists_ref,
    pos_ref,
    q_hbm,
    bank_hbm,
    place_ref,
    home_hbm,
    q,
    keys,
    out,
    arrived,
    back,
    lastq,
    lg,
    wts,
    lastg,
    local_sem,
    z_sem,
    go_send,
    go_recv,
    back_send,
    back_recv,
    ring_send,
    ring_recv,
    sib_send,
    sib_recv,
):
    clu, bank = lax.axis_index("clu"), lax.axis_index("bank")
    x, z = clu // NZ, clu % NZ
    y, core = bank // 2, bank % 2
    sibling = (clu, y * 2 + 1 - core)
    across = (x * NZ + lax.rem(z + 4, NZ), bank)

    def beside(d):
        return (clu, lax.rem(y + (1 if d == 0 else NY - 1), NY) * 2 + core)

    def at(dx, dz):
        return (lax.rem(x + dx, NX) * NZ + lax.rem(z + dz, NZ), bank)

    def remote(src, dst, send, recv, dev):
        return pltpu.make_async_remote_copy(
            src_ref=src, dst_ref=dst, send_sem=send, recv_sem=recv, device_id=dev, device_id_type=MESH
        )

    barrier = pltpu.get_barrier_semaphore()

    def greet(k, _):
        dx, dz = offsets(k, 0)

        @pl.when(k != 0)
        def _():
            pl.semaphore_signal(barrier, inc=1, device_id=at(dx, dz), device_id_type=MESH)

        return 0

    lax.fori_loop(0, NA, greet, 0)
    for dev in (sibling, across, beside(0), beside(1)):
        pl.semaphore_signal(barrier, inc=1, device_id=dev, device_id_type=MESH)

    own = pl.multiple_of((y * 2 + core) * BROWS, BROWS)
    get_q = pltpu.make_async_copy(q_hbm, q, local_sem.at[0])
    get_q.start()
    get_bank = pltpu.make_async_copy(bank_hbm, keys.at[0, pl.ds(own, BROWS)], local_sem.at[1])
    get_bank.start()

    pl.semaphore_wait(barrier, NA - 1 + 4)

    def z_copy(h):
        to = keys.at[1, pl.ds(pl.multiple_of(own + h * HALF, HALF), HALF)]
        return remote(bank_hbm.at[pl.ds(h * HALF, HALF)], to, z_sem.at[0, h], z_sem.at[1, h], across)

    z_copy(0).start()
    z_copy(1).start()

    def rows_of(part, d, s, h):
        src = lax.rem(y + (NY - s if d == 0 else s), NY) * 2 + core
        return keys.at[part, pl.ds(pl.multiple_of(src * BROWS + h * HALF, HALF), HALF)]

    def ring(part, d, s, h):
        ref = rows_of(part, d, s - 1, h)
        src = bank_hbm.at[pl.ds(h * HALF, HALF)] if part == 0 and s == 1 else ref
        return remote(src, ref, ring_send.at[part, d, s - 1, h], ring_recv.at[part, d, s - 1, h], beside(d))

    def to_sibling(part, d, s, h):
        ref = rows_of(part, d, s, h)
        src = bank_hbm.at[pl.ds(h * HALF, HALF)] if part == 0 and s == 0 else ref
        return remote(src, ref, sib_send.at[part, d, s, h], sib_recv.at[part, d, s, h], sibling)

    def halves(s, d):
        return (0, 1) if s < 4 else (d,)

    def ring_begin(part):
        for h in (0, 1):
            if part == 1:
                z_copy(h).wait_recv()
            for d in (0, 1):
                ring(part, d, 1, h).start()
            to_sibling(part, 0, 0, h).start()

    def ring_step(part, s, h):
        for d in (0, 1):
            if h in halves(s, d):
                ring(part, d, s, h).wait_recv()
                if s < 4 and h in halves(s + 1, d):
                    ring(part, d, s + 1, h).start()
                to_sibling(part, d, s, h).start()

    def sibling_done(part, s):
        if s == 0:
            for h in (0, 1):
                to_sibling(part, 0, 0, h).wait_recv()
            return
        for d in (0, 1):
            for h in halves(s, d):
                to_sibling(part, d, s, h).wait_recv()

    def ring_end(part):
        for h in (0, 1):
            to_sibling(part, 0, 0, h).wait_send()
        for s in range(1, 5):
            for d in (0, 1):
                for h in halves(s, d):
                    ring(part, d, s, h).wait_send()
                    to_sibling(part, d, s, h).wait_send()

    ring_begin(0)

    cid = cid_ref[...]
    dx = ((cid >> 3) - x + NX) & (NX - 1)
    dz = ((cid & 7) - z + NZ) & (NZ - 1)
    second = (dz >= 3) & (dz <= 5)
    away = jnp.where(second, dz - 4, jnp.where(dz > 4, dz - NZ, dz))
    turn = jnp.where(away > 0, 2 * away - 1, -2 * away)
    piece = jnp.where(second, NA, 0) + turn * NX + dx
    named = iota((PIECES, QDEV), 0) == piece
    earlier = ones_where(iota((QDEV, QDEV), 0) < iota((QDEV, QDEV), 1))
    rank = jnp.sum(jnp.where(named, dot(ones_where(named), earlier), 0.0), axis=0, keepdims=True)
    rank = rank.astype(jnp.int32)
    slot = piece * ROWS + rank
    slot_last = piece * ROWS + CAP + (rank & 3)
    third = rank >> 2
    place_ref[0:1, :] = slot
    place_ref[1:2, :] = slot_last
    place_ref[2:3, :] = third
    lane = iota((128, QDEV), 0)
    listed = lists_ref[0:1, :] == lane
    for j in range(1, lists_ref.shape[0]):
        listed = listed | (lists_ref[j : j + 1, :] == lane)
    pos = pos_ref[...]
    labels = jnp.where(listed & (lane < 16), 1.0, 0.0)
    labels = jnp.where(lane == 16, (pos >> 6).astype(F32), labels)
    labels = jnp.where(lane == 17, (pos & 63).astype(F32), labels).astype(BF)

    def piece_rows(ref, k):
        return ref.at[pl.ds(pl.multiple_of(k * ROWS, ROWS), ROWS)]

    def go(k, part):
        dx, dz = offsets(k, part)
        return remote(piece_rows(out, k), piece_rows(arrived, k), go_send.at[k], go_recv.at[k], at(dx, dz))

    GROUPS = ((0, PART), (PART, PART), (2 * PART, PART + 128))

    def come(k, part, t):
        dx, dz = offsets(k, part)
        dev = at(lax.rem(NX - dx, NX), lax.rem(NZ - dz, NZ))
        cols = pl.ds(*GROUPS[t])
        src, to = piece_rows(back, k).at[:, cols], piece_rows(home_hbm, k).at[:, cols]
        return remote(src, to, back_send.at[t, k], back_recv.at[t, k], dev)

    SELF = (0, NA)
    stay_go = [
        pltpu.make_async_copy(piece_rows(out, SELF[p]), piece_rows(arrived, SELF[p]), local_sem.at[2 + p])
        for p in (0, 1)
    ]
    stay_come = [
        pltpu.make_async_copy(piece_rows(back, SELF[p]), piece_rows(home_hbm, SELF[p]), local_sem.at[4 + p])
        for p in (0, 1)
    ]

    def each(lo, hi, part, act):
        def step(k, _):
            @pl.when(k != SELF[part])
            def _():
                act(k)

            return 0

        lax.fori_loop(lo, hi, step, 0)

    get_q.wait()

    def pack(base, count):
        row = base + iota((count, QDEV), 0)
        main = ones_where(row == slot)
        out[base : base + count, MAIN:WIDE] = dot_t(main, labels).astype(BF)

        def step(t, _):
            cols = pl.ds(pl.multiple_of(t * PART, 128), PART)
            last = ones_where((row == slot_last) & (third == t))
            out[base : base + count, cols] = (dot(main, q[:, cols]) + dot(last, q[:, MAIN:D])).astype(BF)
            return 0

        lax.fori_loop(0, 3, step, 0)

    for base, count in ((0, 160), (160, 160)):
        pack(base, count)
        each(base // ROWS, (base + count) // ROWS, 0, lambda k: go(k, 0).start())
    stay_go[0].start()
    pack(BASE[1], COUNT[1])

    def gather_last(part):
        base, count = BASE[part], COUNT[part]
        i, j = iota((count, count), 0), iota((count, count), 1)
        total = None
        for t in range(3):
            pick = ones_where((i >> 4 == j >> 4) & ((i & 15) == (j & 15) - CAP + 4 * t) & ((j & 15) >= CAP))
            term = dot(pick, arrived[base : base + count, t * PART : (t + 1) * PART])
            total = term if total is None else total + term
        lastq[base : base + count, :] = total.astype(BF)

    def logits(part, begin, steps, size):
        base, count = BASE[part], COUNT[part]

        def step(j, _):
            rows = pl.ds(pl.multiple_of(lax.rem((begin + j) * size, KEYS), size), size)
            total = dot_t(arrived[base : base + count, 0:MAIN], keys[part, rows, 0:MAIN])
            total = total + dot_t(lastq[base : base + count, :], keys[part, rows, MAIN:D])
            lg[base : base + count, rows] = total * SCALE
            return 0

        lax.fori_loop(0, steps, step, 0)

    def softmax(part):
        base, count = BASE[part], COUNT[part]
        sub = 64
        kblock = iota((128, KEYS), 1) >> 6
        spread = ones_where(kblock == iota((128, KEYS), 0))

        def step(i, _):
            rows = pl.ds(pl.multiple_of(base + i * sub, sub), sub)
            tags = arrived[rows, MAIN:WIDE]
            l = lg[rows, :]
            high = tags[:, 16:17].astype(F32)
            pos = (high * 64.0 + tags[:, 17:18].astype(F32)).astype(jnp.int32)
            key = iota((sub, KEYS), 1)
            allowed = (dot(tags, spread) > 0.5) | (key >> 6 == high.astype(jnp.int32))
            hot = key == pos
            usable = jnp.where(allowed, l, -1e30)
            top = jnp.max(usable, axis=1, keepdims=True)
            e = jnp.exp(usable - top)
            total = jnp.sum(e, axis=1, keepdims=True)
            lse = top + jnp.log(total)
            loss = lse - jnp.sum(jnp.where(hot, l, 0.0), axis=1, keepdims=True)
            probs = (e * (1.0 / total)).astype(BF).astype(F32)
            wts[rows, :] = jnp.where(hot, probs - 1.0, probs).astype(BF)
            back[rows, MAIN:WIDE] = jnp.where(iota((sub, 128), 1) == 0, loss, 0.0).astype(BF)
            return 0

        lax.fori_loop(0, count // sub, step, 0)

    def pull(part, sent):
        base, count = BASE[part], COUNT[part]
        lastg[0:count, :] = (dot(wts[base : base + count, :], keys[part, :, MAIN:D]) * SCALE).astype(BF)
        i, j = iota((count, count), 0), iota((count, count), 1)
        upper = iota((count, 1), 0) & 15

        for t in range(3):
            cols = slice(t * PART, (t + 1) * PART)
            main = dot(wts[base : base + count, :], keys[part, :, cols]) * SCALE
            put = ones_where((i >> 4 == j >> 4) & ((i & 15) >= CAP) & ((j & 15) == (i & 15) - CAP + 4 * t))
            low = dot(put, lastg[0:count, :])
            back[base : base + count, cols] = jnp.where(upper < CAP, main, low).astype(BF)
            sent(t)

    for s, h in ((1, 0), (1, 1), (2, 0), (2, 1), (3, 0), (3, 1)):
        ring_step(0, s, h)
    ring_begin(1)
    ring_step(0, 4, 0)
    ring_step(0, 4, 1)
    for i in range(5):
        sibling_done(0, i)
    get_bank.wait()

    each(0, NA, 0, lambda k: go(k, 0).wait_recv())
    stay_go[0].wait()
    each(NA, PIECES, 1, lambda k: go(k, 1).start())
    stay_go[1].start()
    gather_last(0)
    ring_step(1, 1, 0)
    logits(0, 0, KEYS // KTILE, KTILE)
    ring_step(1, 1, 1)
    softmax(0)
    ring_step(1, 2, 0)

    def sent_first(t):
        each(0, NA, 0, lambda k: come(k, 0, t).start())
        if t == 2:
            stay_come[0].start()

    pull(0, sent_first)
    ring_step(1, 2, 1)
    each(NA, PIECES, 1, lambda k: go(k, 1).wait_recv())
    stay_go[1].wait()
    gather_last(1)
    ring_step(1, 3, 0)
    ring_step(1, 3, 1)
    for i in range(3):
        sibling_done(1, i)
    logits(1, y + NY - 2, 5, 2 * BROWS)
    sibling_done(1, 3)
    logits(1, y + 3, 1, 2 * BROWS)
    logits(1, y + 5, 1, 2 * BROWS)
    ring_step(1, 4, 0)
    ring_step(1, 4, 1)
    sibling_done(1, 4)

    logits(1, y + 4, 1, 2 * BROWS)
    softmax(1)

    def sent_second(t):
        each(NA, PIECES, 1, lambda k: come(k, 1, t).start())
        if t == 2:
            stay_come[1].start()

    pull(1, sent_second)
    ring_end(0)
    ring_end(1)
    z_copy(0).wait_send()
    z_copy(1).wait_send()
    each(0, NA, 0, lambda k: go(k, 0).wait_send())
    each(NA, PIECES, 1, lambda k: go(k, 1).wait_send())

    stay_come[0].wait()
    stay_come[1].wait()
    for t in range(3):
        each(0, NA, 0, lambda k: come(k, 0, t).wait_send())
        each(0, NA, 0, lambda k: come(k, 0, t).wait_recv())
    for t in range(3):
        each(NA, PIECES, 1, lambda k: come(k, 1, t).wait_send())
        each(NA, PIECES, 1, lambda k: come(k, 1, t).wait_recv())


def finish(place_ref, weight_ref, home_hbm, grad_hbm, loss_ref, home, grad, in_sem, out_sem):
    def get(t):
        cols = pl.ds(t * PART, PART) if t < 3 else pl.ds(MAIN, 128)
        return pltpu.make_async_copy(home_hbm.at[:, cols], home.at[:, cols], in_sem.at[t])

    def put(t):
        cols = pl.ds(t * PART, PART)
        return pltpu.make_async_copy(grad.at[:, cols], grad_hbm.at[:, cols], out_sem.at[t])

    for t in range(4):
        get(t).start()
    eye = iota((QDEV, QDEV), 0) == iota((QDEV, QDEV), 1)

    def to_row(col):
        return jnp.sum(jnp.where(eye, col, 0.0), axis=0, keepdims=True)

    def to_col(row):
        return jnp.sum(jnp.where(eye, row, 0.0), axis=1, keepdims=True)

    slot, slot_last, third = [to_col(place_ref[i : i + 1, :].astype(F32)).astype(jnp.int32) for i in range(3)]
    weight = to_col(weight_ref[...])
    col = iota((QDEV, PIECES * ROWS), 1)
    main = ones_where(slot == col)
    total = None
    for t in range(3):
        cols = slice(t * PART, (t + 1) * PART)
        get(t).wait()
        grad[:, cols] = (dot(main, home[:, cols]) * weight).astype(BF)
        put(t).start()
        term = dot(ones_where((slot_last == col) & (third == t)), home[:, cols])
        total = term if total is None else total + term
    grad[:, MAIN:D] = (total * weight).astype(BF)
    put(3).start()
    get(3).wait()
    losses = dot(main, home[:, MAIN:WIDE])
    loss_ref[...] = to_row(losses[:, 0:1]).reshape(QDEV).astype(BF)
    for t in range(4):
        put(t).wait()


def body(queries, bank, cluster_ids, block_lists, positive_ids, loss_weights):
    vmem = pl.BlockSpec(memory_space=pltpu.VMEM)
    hbm = pl.BlockSpec(memory_space=pl.ANY)
    dma = pltpu.SemaphoreType.DMA
    slots = (PIECES * ROWS, WIDE)
    place, home = pl.pallas_call(
        kernel,
        out_shape=(
            jax.ShapeDtypeStruct((8, QDEV), jnp.int32),
            jax.ShapeDtypeStruct(slots, BF),
        ),
        in_specs=[vmem, vmem, vmem, hbm, hbm],
        out_specs=(vmem, hbm),
        scratch_shapes=[
            pltpu.VMEM((QDEV, D), BF),
            pltpu.VMEM((2, KEYS, D), BF),
            pltpu.VMEM(slots, BF),
            pltpu.VMEM(slots, BF),
            pltpu.VMEM(slots, BF),
            pltpu.VMEM((PIECES * ROWS, PART), BF),
            pltpu.VMEM((PIECES * ROWS, KEYS), F32),
            pltpu.VMEM((PIECES * ROWS, KEYS), BF),
            pltpu.VMEM((COUNT[0], PART), BF),
            dma((6,)),
            dma((2, 2)),
            dma((PIECES,)),
            dma((PIECES,)),
            dma((3, PIECES)),
            dma((3, PIECES)),
            dma((2, 2, 4, 2)),
            dma((2, 2, 4, 2)),
            dma((2, 2, 5, 2)),
            dma((2, 2, 5, 2)),
        ],
        compiler_params=pltpu.CompilerParams(
            collective_id=0, has_side_effects=True, vmem_limit_bytes=60 * 1024 * 1024
        ),
        cost_estimate=pl.CostEstimate(flops=10**10, bytes_accessed=10**7, transcendentals=10**6),
    )(cluster_ids.reshape(1, QDEV), block_lists.T, positive_ids.reshape(1, QDEV), queries, bank)
    grad, loss = pl.pallas_call(
        finish,
        out_shape=(jax.ShapeDtypeStruct((QDEV, D), BF), jax.ShapeDtypeStruct((QDEV,), BF)),
        in_specs=[vmem, vmem, hbm],
        out_specs=(hbm, vmem),
        scratch_shapes=[
            pltpu.VMEM(slots, BF),
            pltpu.VMEM((QDEV, D), BF),
            dma((4,)),
            dma((4,)),
        ],
        compiler_params=pltpu.CompilerParams(vmem_limit_bytes=60 * 1024 * 1024),
        cost_estimate=pl.CostEstimate(flops=10**9, bytes_accessed=5 * 10**6, transcendentals=0),
    )(place, loss_weights.reshape(1, QDEV), home)
    return grad, loss


def solution(mesh):
    rows = P(("clu", "bank"), None)
    flat = P(("clu", "bank"))
    return jax.shard_map(
        body,
        mesh=mesh,
        in_specs=(rows, rows, rows, rows, flat, flat),
        out_specs=(rows, flat),
        check_vma=False,
    )
```

```python
import functools
import math

import jax
import jax.numpy as jnp
from jax import lax
from jax.experimental import pallas as pl
from jax.experimental.pallas import tpu as pltpu
from jax.sharding import PartitionSpec as P

MESH = pl.DeviceIdType.MESH
D = 3584
NX, NZ, NY = 4, 8, 8
NA, NB = 20, 12
PIECES = NA + NB
CAP = 12
ROWS = 16
PART = 896
MAIN = 3 * PART
WIDE = MAIN + 128
QDEV = 256
BROWS = 64
HALF = BROWS // 2
KEYS = 1024
KTILE = 256
BASE = (0, NA * ROWS)
COUNT = (NA * ROWS, NB * ROWS)
SCALE = 3.0 / math.sqrt(D)
BF = jnp.bfloat16
F32 = jnp.float32


def dot(a, b):
    return jnp.dot(a, b, preferred_element_type=F32)


def dot_t(a, b):
    return lax.dot_general(a, b, (((1,), (1,)), ((), ())), preferred_element_type=F32)


def iota(shape, dim):
    return lax.broadcasted_iota(jnp.int32, shape, dim)


def ones_where(cond):
    return jnp.where(cond, 1.0, 0.0).astype(BF)


def offsets(k, part):
    k = k - part * NA
    turn, dx = k // NX, k % NX
    odd = turn % 2
    return dx, odd * ((turn + 1) // 2) + (1 - odd) * lax.rem(NZ - turn // 2, NZ)


def kernel(
    cid_ref,
    lists_ref,
    pos_ref,
    weight_ref,
    q_hbm,
    bank_hbm,
    place_ref,
    home_hbm,
    q,
    keys,
    out,
    arrived,
    back,
    lastq,
    lg,
    wts,
    lastg,
    local_sem,
    z_sem,
    go_send,
    go_recv,
    back_send,
    back_recv,
    ring_send,
    ring_recv,
    sib_send,
    sib_recv,
):
    clu, bank = lax.axis_index("clu"), lax.axis_index("bank")
    x, z = clu // NZ, clu % NZ
    y, core = bank // 2, bank % 2
    sibling = (clu, y * 2 + 1 - core)
    across = (x * NZ + lax.rem(z + 4, NZ), bank)

    def beside(d):
        return (clu, lax.rem(y + (1 if d == 0 else NY - 1), NY) * 2 + core)

    def at(dx, dz):
        return (lax.rem(x + dx, NX) * NZ + lax.rem(z + dz, NZ), bank)

    def remote(src, dst, send, recv, dev):
        return pltpu.make_async_remote_copy(
            src_ref=src, dst_ref=dst, send_sem=send, recv_sem=recv, device_id=dev, device_id_type=MESH
        )

    barrier = pltpu.get_barrier_semaphore()

    def greet(k, _):
        dx, dz = offsets(k, 0)

        @pl.when(k != 0)
        def _():
            pl.semaphore_signal(barrier, inc=1, device_id=at(dx, dz), device_id_type=MESH)

        return 0

    lax.fori_loop(0, NA, greet, 0)
    for dev in (sibling, across, beside(0), beside(1)):
        pl.semaphore_signal(barrier, inc=1, device_id=dev, device_id_type=MESH)

    own = pl.multiple_of((y * 2 + core) * BROWS, BROWS)
    get_q = pltpu.make_async_copy(q_hbm, q, local_sem.at[0])
    get_q.start()
    get_bank = pltpu.make_async_copy(bank_hbm, keys.at[0, pl.ds(own, BROWS)], local_sem.at[1])
    get_bank.start()

    pl.semaphore_wait(barrier, NA - 1 + 4)

    def z_copy(h):
        to = keys.at[1, pl.ds(pl.multiple_of(own + h * HALF, HALF), HALF)]
        return remote(bank_hbm.at[pl.ds(h * HALF, HALF)], to, z_sem.at[0, h], z_sem.at[1, h], across)

    z_copy(0).start()
    z_copy(1).start()

    def rows_of(part, d, s, h):
        src = lax.rem(y + (NY - s if d == 0 else s), NY) * 2 + core
        return keys.at[part, pl.ds(pl.multiple_of(src * BROWS + h * HALF, HALF), HALF)]

    def ring(part, d, s, h):
        ref = rows_of(part, d, s - 1, h)
        src = bank_hbm.at[pl.ds(h * HALF, HALF)] if part == 0 and s == 1 else ref
        return remote(src, ref, ring_send.at[part, d, s - 1, h], ring_recv.at[part, d, s - 1, h], beside(d))

    def to_sibling(part, d, s, h):
        ref = rows_of(part, d, s, h)
        src = bank_hbm.at[pl.ds(h * HALF, HALF)] if part == 0 and s == 0 else ref
        return remote(src, ref, sib_send.at[part, d, s, h], sib_recv.at[part, d, s, h], sibling)

    def halves(s, d):
        return (0, 1) if s < 4 else (d,)

    def ring_begin(part):
        for h in (0, 1):
            if part == 1:
                z_copy(h).wait_recv()
            for d in (0, 1):
                ring(part, d, 1, h).start()
            to_sibling(part, 0, 0, h).start()

    def ring_step(part, s, h):
        for d in (0, 1):
            if h in halves(s, d):
                ring(part, d, s, h).wait_recv()
                if s < 4 and h in halves(s + 1, d):
                    ring(part, d, s + 1, h).start()
                to_sibling(part, d, s, h).start()

    def sibling_done(part, s):
        if s == 0:
            for h in (0, 1):
                to_sibling(part, 0, 0, h).wait_recv()
            return
        for d in (0, 1):
            for h in halves(s, d):
                to_sibling(part, d, s, h).wait_recv()

    def ring_end(part):
        for h in (0, 1):
            to_sibling(part, 0, 0, h).wait_send()
        for s in range(1, 5):
            for d in (0, 1):
                for h in halves(s, d):
                    ring(part, d, s, h).wait_send()
                    to_sibling(part, d, s, h).wait_send()

    ring_begin(0)

    cid = cid_ref[...]
    dx = ((cid >> 3) - x + NX) & (NX - 1)
    dz = ((cid & 7) - z + NZ) & (NZ - 1)
    second = (dz >= 3) & (dz <= 5)
    away = jnp.where(second, dz - 4, jnp.where(dz > 4, dz - NZ, dz))
    turn = jnp.where(away > 0, 2 * away - 1, -2 * away)
    piece = jnp.where(second, NA, 0) + turn * NX + dx
    named = iota((PIECES, QDEV), 0) == piece
    earlier = ones_where(iota((QDEV, QDEV), 0) < iota((QDEV, QDEV), 1))
    rank = jnp.sum(jnp.where(named, dot(ones_where(named), earlier), 0.0), axis=0, keepdims=True)
    rank = rank.astype(jnp.int32)
    slot = piece * ROWS + rank
    slot_last = piece * ROWS + CAP + (rank & 3)
    third = rank >> 2
    lane = iota((128, QDEV), 0)
    listed = lists_ref[0:1, :] == lane
    for j in range(1, lists_ref.shape[0]):
        listed = listed | (lists_ref[j : j + 1, :] == lane)
    pos = pos_ref[...]
    labels = jnp.where(listed & (lane < 16), 1.0, 0.0)
    labels = jnp.where(lane == 16, (pos >> 6).astype(F32), labels)
    labels = jnp.where(lane == 17, (pos & 63).astype(F32), labels).astype(BF)

    def piece_rows(ref, k):
        return ref.at[pl.ds(pl.multiple_of(k * ROWS, ROWS), ROWS)]

    def go(k, part):
        dx, dz = offsets(k, part)
        return remote(piece_rows(out, k), piece_rows(arrived, k), go_send.at[part], go_recv.at[part], at(dx, dz))

    GROUPS = ((0, PART), (PART, PART), (2 * PART, PART + 128))

    def come(k, part, t):
        dx, dz = offsets(k, part)
        dev = at(lax.rem(NX - dx, NX), lax.rem(NZ - dz, NZ))
        cols = pl.ds(*GROUPS[t])
        src, to = piece_rows(back, k).at[:, cols], piece_rows(home_hbm, k).at[:, cols]
        return remote(src, to, back_send.at[part], back_recv.at[part], dev)

    def others(ref, part):
        return ref.at[pl.ds(BASE[part] + ROWS, COUNT[part] - ROWS)]

    def all_go(part):
        return remote(others(out, part), others(arrived, part), go_send.at[part], go_recv.at[part], sibling)

    def all_come(part):
        return remote(others(back, part), others(home_hbm, part), back_send.at[part], back_recv.at[part], sibling)

    SELF = (0, NA)
    stay_go = [
        pltpu.make_async_copy(piece_rows(out, SELF[p]), piece_rows(arrived, SELF[p]), local_sem.at[2 + p])
        for p in (0, 1)
    ]
    stay_come = [
        pltpu.make_async_copy(piece_rows(back, SELF[p]), piece_rows(home_hbm, SELF[p]), local_sem.at[4 + p])
        for p in (0, 1)
    ]

    def each(lo, hi, part, act):
        def step(k, _):
            @pl.when(k != SELF[part])
            def _():
                act(k)

            return 0

        lax.fori_loop(lo, hi, step, 0)

    get_q.wait()

    def pack(base, count):
        row = base + iota((count, QDEV), 0)
        main = ones_where(row == slot)
        out[base : base + count, MAIN:WIDE] = dot_t(main, labels).astype(BF)

        def step(t, _):
            cols = pl.ds(pl.multiple_of(t * PART, 128), PART)
            last = ones_where((row == slot_last) & (third == t))
            out[base : base + count, cols] = (dot(main, q[:, cols]) + dot(last, q[:, MAIN:D])).astype(BF)
            return 0

        lax.fori_loop(0, 3, step, 0)

    for base, count in ((0, 160), (160, 160)):
        pack(base, count)
        each(base // ROWS, (base + count) // ROWS, 0, lambda k: go(k, 0).start())
    stay_go[0].start()
    pack(BASE[1], COUNT[1])

    def gather_last(part):
        base, count = BASE[part], COUNT[part]
        i, j = iota((count, count), 0), iota((count, count), 1)
        total = None
        for t in range(3):
            pick = ones_where((i >> 4 == j >> 4) & ((i & 15) == (j & 15) - CAP + 4 * t) & ((j & 15) >= CAP))
            term = dot(pick, arrived[base : base + count, t * PART : (t + 1) * PART])
            total = term if total is None else total + term
        lastq[base : base + count, :] = total.astype(BF)

    def logits(part, begin, steps, size):
        base, count = BASE[part], COUNT[part]

        def step(j, _):
            rows = pl.ds(pl.multiple_of(lax.rem((begin + j) * size, KEYS), size), size)
            total = dot_t(arrived[base : base + count, 0:MAIN], keys[part, rows, 0:MAIN])
            total = total + dot_t(lastq[base : base + count, :], keys[part, rows, MAIN:D])
            lg[base : base + count, rows] = total * SCALE
            return 0

        lax.fori_loop(0, steps, step, 0)

    def softmax(part):
        base, count = BASE[part], COUNT[part]
        sub = 64
        kblock = iota((128, KEYS), 1) >> 6
        spread = ones_where(kblock == iota((128, KEYS), 0))

        def step(i, _):
            rows = pl.ds(pl.multiple_of(base + i * sub, sub), sub)
            tags = arrived[rows, MAIN:WIDE]
            l = lg[rows, :]
            high = tags[:, 16:17].astype(F32)
            pos = (high * 64.0 + tags[:, 17:18].astype(F32)).astype(jnp.int32)
            key = iota((sub, KEYS), 1)
            allowed = (dot(tags, spread) > 0.5) | (key >> 6 == high.astype(jnp.int32))
            hot = key == pos
            usable = jnp.where(allowed, l, -1e30)
            top = jnp.max(usable, axis=1, keepdims=True)
            e = jnp.exp(usable - top)
            total = jnp.sum(e, axis=1, keepdims=True)
            lse = top + jnp.log(total)
            loss = lse - jnp.sum(jnp.where(hot, l, 0.0), axis=1, keepdims=True)
            probs = (e * (1.0 / total)).astype(BF).astype(F32)
            wts[rows, :] = jnp.where(hot, probs - 1.0, probs).astype(BF)
            back[rows, MAIN:WIDE] = jnp.where(iota((sub, 128), 1) == 0, loss, 0.0).astype(BF)
            return 0

        lax.fori_loop(0, count // sub, step, 0)

    def pull(part, sent):
        base, count = BASE[part], COUNT[part]
        lastg[0:count, :] = (dot(wts[base : base + count, :], keys[part, :, MAIN:D]) * SCALE).astype(BF)
        i, j = iota((count, count), 0), iota((count, count), 1)
        upper = iota((count, 1), 0) & 15

        for t in range(3):
            cols = slice(t * PART, (t + 1) * PART)
            main = dot(wts[base : base + count, :], keys[part, :, cols]) * SCALE
            put = ones_where((i >> 4 == j >> 4) & ((i & 15) >= CAP) & ((j & 15) == (i & 15) - CAP + 4 * t))
            low = dot(put, lastg[0:count, :])
            back[base : base + count, cols] = jnp.where(upper < CAP, main, low).astype(BF)
            sent(t)

    for s, h in ((1, 0), (1, 1), (2, 0), (2, 1), (3, 0), (3, 1)):
        ring_step(0, s, h)
    ring_begin(1)
    ring_step(0, 4, 0)
    ring_step(0, 4, 1)
    for i in range(5):
        sibling_done(0, i)
    get_bank.wait()

    all_go(0).wait_recv()
    stay_go[0].wait()
    each(NA, PIECES, 1, lambda k: go(k, 1).start())
    stay_go[1].start()
    gather_last(0)
    ring_step(1, 1, 0)
    logits(0, 0, KEYS // KTILE, KTILE)
    ring_step(1, 1, 1)
    softmax(0)
    ring_step(1, 2, 0)

    def sent_first(t):
        each(0, NA, 0, lambda k: come(k, 0, t).start())
        if t == 2:
            stay_come[0].start()

    pull(0, sent_first)
    ring_step(1, 2, 1)
    all_go(1).wait_recv()
    stay_go[1].wait()
    gather_last(1)
    ring_step(1, 3, 0)
    ring_step(1, 3, 1)
    eye = iota((QDEV, QDEV), 0) == iota((QDEV, QDEV), 1)
    lane = iota((QDEV, 128), 1)
    for i, row in enumerate((slot.astype(F32), slot_last.astype(F32), third.astype(F32), weight_ref[...])):
        column = jnp.sum(jnp.where(eye, row, 0.0), axis=1, keepdims=True)
        place_ref[...] = jnp.where(lane == i, column, 0.0 if i == 0 else place_ref[...])
    for i in range(3):
        sibling_done(1, i)
    logits(1, y + NY - 2, 5, 2 * BROWS)
    sibling_done(1, 3)
    logits(1, y + 3, 1, 2 * BROWS)
    logits(1, y + 5, 1, 2 * BROWS)
    ring_end(0)
    ring_step(1, 4, 0)
    ring_step(1, 4, 1)
    sibling_done(1, 4)

    logits(1, y + 4, 1, 2 * BROWS)
    softmax(1)

    def sent_second(t):
        each(NA, PIECES, 1, lambda k: come(k, 1, t).start())
        if t == 2:
            stay_come[1].start()

    pull(1, sent_second)
    ring_end(1)
    z_copy(0).wait_send()
    z_copy(1).wait_send()
    all_go(0).wait_send()
    all_go(1).wait_send()

    stay_come[0].wait()
    stay_come[1].wait()
    for part in (0, 1):
        all_come(part).wait_send()
        all_come(part).wait_recv()


def finish(place_ref, home_hbm, grad_hbm, loss_ref, home, grad, in_sem, out_sem):
    def get(t):
        cols = pl.ds(t * PART, PART) if t < 3 else pl.ds(MAIN, 128)
        return pltpu.make_async_copy(home_hbm.at[:, cols], home.at[:, cols], in_sem.at[t])

    def put(t):
        cols = pl.ds(t * PART, PART)
        return pltpu.make_async_copy(grad.at[:, cols], grad_hbm.at[:, cols], out_sem.at[t])

    for t in range(4):
        get(t).start()
    slot, slot_last, third = [place_ref[:, i : i + 1].astype(jnp.int32) for i in range(3)]
    weight = place_ref[:, 3:4]
    col = iota((QDEV, PIECES * ROWS), 1)
    main = ones_where(slot == col)
    total = None
    for t in range(3):
        cols = slice(t * PART, (t + 1) * PART)
        get(t).wait()
        both = jnp.concatenate([main, ones_where((slot_last == col) & (third == t))], axis=0)
        moved = dot(both, home[:, cols])
        grad[:, cols] = (moved[:QDEV] * weight).astype(BF)
        put(t).start()
        term = moved[QDEV:]
        total = term if total is None else total + term
    grad[:, MAIN:D] = (total * weight).astype(BF)
    put(3).start()
    get(3).wait()
    losses = dot(main, home[:, MAIN:WIDE])
    eye = iota((QDEV, QDEV), 0) == iota((QDEV, QDEV), 1)
    loss_ref[...] = jnp.sum(jnp.where(eye, losses[:, 0:1], 0.0), axis=0, keepdims=True).reshape(QDEV).astype(BF)
    for t in range(4):
        put(t).wait()


def body(queries, bank, cluster_ids, block_lists, positive_ids, loss_weights):
    vmem = pl.BlockSpec(memory_space=pltpu.VMEM)
    hbm = pl.BlockSpec(memory_space=pl.ANY)
    dma = pltpu.SemaphoreType.DMA
    slots = (PIECES * ROWS, WIDE)
    place, home = pl.pallas_call(
        kernel,
        out_shape=(
            jax.ShapeDtypeStruct((QDEV, 128), F32),
            jax.ShapeDtypeStruct(slots, BF),
        ),
        in_specs=[vmem, vmem, vmem, vmem, hbm, hbm],
        out_specs=(vmem, hbm),
        scratch_shapes=[
            pltpu.VMEM((QDEV, D), BF),
            pltpu.VMEM((2, KEYS, D), BF),
            pltpu.VMEM(slots, BF),
            pltpu.VMEM(slots, BF),
            pltpu.VMEM(slots, BF),
            pltpu.VMEM((PIECES * ROWS, PART), BF),
            pltpu.VMEM((PIECES * ROWS, KEYS), F32),
            pltpu.VMEM((PIECES * ROWS, KEYS), BF),
            pltpu.VMEM((COUNT[0], PART), BF),
            dma((6,)),
            dma((2, 2)),
            dma((2,)),
            dma((2,)),
            dma((2,)),
            dma((2,)),
            dma((2, 2, 4, 2)),
            dma((2, 2, 4, 2)),
            dma((2, 2, 5, 2)),
            dma((2, 2, 5, 2)),
        ],
        compiler_params=pltpu.CompilerParams(
            collective_id=0, has_side_effects=True, vmem_limit_bytes=60 * 1024 * 1024
        ),
        cost_estimate=pl.CostEstimate(flops=10**10, bytes_accessed=10**7, transcendentals=10**6),
    )(
        cluster_ids.reshape(1, QDEV),
        block_lists.T,
        positive_ids.reshape(1, QDEV),
        loss_weights.reshape(1, QDEV),
        queries,
        bank,
    )
    grad, loss = pl.pallas_call(
        finish,
        out_shape=(jax.ShapeDtypeStruct((QDEV, D), BF), jax.ShapeDtypeStruct((QDEV,), BF)),
        in_specs=[vmem, hbm],
        out_specs=(hbm, vmem),
        scratch_shapes=[
            pltpu.VMEM(slots, BF),
            pltpu.VMEM((QDEV, D), BF),
            dma((4,)),
            dma((4,)),
        ],
        compiler_params=pltpu.CompilerParams(vmem_limit_bytes=60 * 1024 * 1024),
        cost_estimate=pl.CostEstimate(flops=10**9, bytes_accessed=5 * 10**6, transcendentals=0),
    )(place, home)
    return grad, loss


def solution(mesh):
    rows = P(("clu", "bank"), None)
    flat = P(("clu", "bank"))
    return jax.shard_map(
        body,
        mesh=mesh,
        in_specs=(rows, rows, rows, rows, flat, flat),
        out_specs=(rows, flat),
        check_vma=False,
    )
```

```python
import functools
import math

import jax
import jax.numpy as jnp
from jax import lax
from jax.experimental import pallas as pl
from jax.experimental.pallas import tpu as pltpu
from jax.sharding import PartitionSpec as P

MESH = pl.DeviceIdType.MESH
D = 3584
NX, NZ, NY = 4, 8, 8
NA, NB = 20, 12
PIECES = NA + NB
CAP = 12
ROWS = 16
PART = 896
MAIN = 3 * PART
WIDE = MAIN + 128
QDEV = 256
BROWS = 64
HALF = BROWS // 2
KEYS = 1024
KTILE = 256
BASE = (0, NA * ROWS)
COUNT = (NA * ROWS, NB * ROWS)
SCALE = 3.0 / math.sqrt(D)
BF = jnp.bfloat16
F32 = jnp.float32


def dot(a, b):
    return jnp.dot(a, b, preferred_element_type=F32)


def dot_t(a, b):
    return lax.dot_general(a, b, (((1,), (1,)), ((), ())), preferred_element_type=F32)


def iota(shape, dim):
    return lax.broadcasted_iota(jnp.int32, shape, dim)


def ones_where(cond):
    return jnp.where(cond, 1.0, 0.0).astype(BF)


def offsets(k, part):
    k = k - part * NA
    turn, dx = k // NX, k % NX
    odd = turn % 2
    return dx, odd * ((turn + 1) // 2) + (1 - odd) * lax.rem(NZ - turn // 2, NZ)


def kernel(
    cid_ref,
    lists_ref,
    pos_ref,
    weight_ref,
    q_hbm,
    bank_hbm,
    place_hbm,
    home_hbm,
    q,
    keys,
    out,
    arrived,
    back,
    lastq,
    lg,
    wts,
    lastg,
    place,
    local_sem,
    z_sem,
    go_send,
    go_recv,
    back_send,
    back_recv,
    ring_send,
    ring_recv,
    sib_send,
    sib_recv,
):
    clu, bank = lax.axis_index("clu"), lax.axis_index("bank")
    x, z = clu // NZ, clu % NZ
    y, core = bank // 2, bank % 2
    sibling = (clu, y * 2 + 1 - core)
    across = (x * NZ + lax.rem(z + 4, NZ), bank)

    def beside(d):
        return (clu, lax.rem(y + (1 if d == 0 else NY - 1), NY) * 2 + core)

    def at(dx, dz):
        return (lax.rem(x + dx, NX) * NZ + lax.rem(z + dz, NZ), bank)

    def remote(src, dst, send, recv, dev):
        return pltpu.make_async_remote_copy(
            src_ref=src, dst_ref=dst, send_sem=send, recv_sem=recv, device_id=dev, device_id_type=MESH
        )

    barrier = pltpu.get_barrier_semaphore()

    def greet(k, _):
        dx, dz = offsets(k, 0)

        @pl.when(k != 0)
        def _():
            pl.semaphore_signal(barrier, inc=1, device_id=at(dx, dz), device_id_type=MESH)

        return 0

    lax.fori_loop(0, NA, greet, 0)
    for dev in (sibling, across, beside(0), beside(1)):
        pl.semaphore_signal(barrier, inc=1, device_id=dev, device_id_type=MESH)

    own = pl.multiple_of((y * 2 + core) * BROWS, BROWS)
    get_q = pltpu.make_async_copy(q_hbm, q, local_sem.at[0])
    get_q.start()
    get_bank = pltpu.make_async_copy(bank_hbm, keys.at[0, pl.ds(own, BROWS)], local_sem.at[1])
    get_bank.start()

    pl.semaphore_wait(barrier, NA - 1 + 4)

    def z_copy(h):
        to = keys.at[1, pl.ds(pl.multiple_of(own + h * HALF, HALF), HALF)]
        return remote(bank_hbm.at[pl.ds(h * HALF, HALF)], to, z_sem.at[0, h], z_sem.at[1, h], across)

    z_copy(0).start()
    z_copy(1).start()

    def rows_of(part, d, s, h):
        src = lax.rem(y + (NY - s if d == 0 else s), NY) * 2 + core
        return keys.at[part, pl.ds(pl.multiple_of(src * BROWS + h * HALF, HALF), HALF)]

    def ring(part, d, s, h):
        ref = rows_of(part, d, s - 1, h)
        src = bank_hbm.at[pl.ds(h * HALF, HALF)] if part == 0 and s == 1 else ref
        return remote(src, ref, ring_send.at[part, d, s - 1, h], ring_recv.at[part, d, s - 1, h], beside(d))

    def to_sibling(part, d, s, h):
        ref = rows_of(part, d, s, h)
        src = bank_hbm.at[pl.ds(h * HALF, HALF)] if part == 0 and s == 0 else ref
        return remote(src, ref, sib_send.at[part, d, s, h], sib_recv.at[part, d, s, h], sibling)

    def halves(s, d):
        return (0, 1) if s < 4 else (d,)

    def ring_begin(part):
        for h in (0, 1):
            if part == 1:
                z_copy(h).wait_recv()
            for d in (0, 1):
                ring(part, d, 1, h).start()
            to_sibling(part, 0, 0, h).start()

    def ring_step(part, s, h):
        for d in (0, 1):
            if h in halves(s, d):
                ring(part, d, s, h).wait_recv()
                if s < 4 and h in halves(s + 1, d):
                    ring(part, d, s + 1, h).start()
                to_sibling(part, d, s, h).start()

    def sibling_done(part, s):
        if s == 0:
            for h in (0, 1):
                to_sibling(part, 0, 0, h).wait_recv()
            return
        for d in (0, 1):
            for h in halves(s, d):
                to_sibling(part, d, s, h).wait_recv()

    def ring_end(part):
        for h in (0, 1):
            to_sibling(part, 0, 0, h).wait_send()
        for s in range(1, 5):
            for d in (0, 1):
                for h in halves(s, d):
                    ring(part, d, s, h).wait_send()
                    to_sibling(part, d, s, h).wait_send()

    ring_begin(0)

    cid = cid_ref[...]
    dx = ((cid >> 3) - x + NX) & (NX - 1)
    dz = ((cid & 7) - z + NZ) & (NZ - 1)
    second = (dz >= 3) & (dz <= 5)
    away = jnp.where(second, dz - 4, jnp.where(dz > 4, dz - NZ, dz))
    turn = jnp.where(away > 0, 2 * away - 1, -2 * away)
    piece = jnp.where(second, NA, 0) + turn * NX + dx
    named = iota((PIECES, QDEV), 0) == piece
    earlier = ones_where(iota((QDEV, QDEV), 0) < iota((QDEV, QDEV), 1))
    rank = jnp.sum(jnp.where(named, dot(ones_where(named), earlier), 0.0), axis=0, keepdims=True)
    rank = rank.astype(jnp.int32)
    slot = piece * ROWS + rank
    slot_last = piece * ROWS + CAP + (rank & 3)
    third = rank >> 2
    lane = iota((128, QDEV), 0)
    listed = lists_ref[0:1, :] == lane
    for j in range(1, lists_ref.shape[0]):
        listed = listed | (lists_ref[j : j + 1, :] == lane)
    pos = pos_ref[...]
    labels = jnp.where(listed & (lane < 16), 1.0, 0.0)
    labels = jnp.where(lane == 16, (pos >> 6).astype(F32), labels)
    labels = jnp.where(lane == 17, (pos & 63).astype(F32), labels).astype(BF)

    def piece_rows(ref, k):
        return ref.at[pl.ds(pl.multiple_of(k * ROWS, ROWS), ROWS)]

    def go(k, part):
        dx, dz = offsets(k, part)
        return remote(piece_rows(out, k), piece_rows(arrived, k), go_send.at[part], go_recv.at[part], at(dx, dz))

    GROUPS = ((0, PART), (PART, PART), (2 * PART, PART + 128))

    def come(k, part, t):
        dx, dz = offsets(k, part)
        dev = at(lax.rem(NX - dx, NX), lax.rem(NZ - dz, NZ))
        cols = pl.ds(*GROUPS[t])
        src, to = piece_rows(back, k).at[:, cols], piece_rows(home_hbm, k).at[:, cols]
        return remote(src, to, back_send.at[part], back_recv.at[part], dev)

    def others(ref, part):
        return ref.at[pl.ds(BASE[part] + ROWS, COUNT[part] - ROWS)]

    def all_go(part):
        return remote(others(out, part), others(arrived, part), go_send.at[part], go_recv.at[part], sibling)

    def all_come(part):
        return remote(others(back, part), others(home_hbm, part), back_send.at[part], back_recv.at[part], sibling)

    SELF = (0, NA)
    stay_go = [
        pltpu.make_async_copy(piece_rows(out, SELF[p]), piece_rows(arrived, SELF[p]), local_sem.at[2 + p])
        for p in (0, 1)
    ]
    stay_come = [
        pltpu.make_async_copy(piece_rows(back, SELF[p]), piece_rows(home_hbm, SELF[p]), local_sem.at[4 + p])
        for p in (0, 1)
    ]

    def each(lo, hi, part, act):
        def step(k, _):
            @pl.when(k != SELF[part])
            def _():
                act(k)

            return 0

        lax.fori_loop(lo, hi, step, 0)

    get_q.wait()

    def pack(base, count):
        row = base + iota((count, QDEV), 0)
        main = ones_where(row == slot)
        out[base : base + count, MAIN:WIDE] = dot_t(main, labels).astype(BF)

        def step(t, _):
            cols = pl.ds(pl.multiple_of(t * PART, 128), PART)
            last = ones_where((row == slot_last) & (third == t))
            out[base : base + count, cols] = (dot(main, q[:, cols]) + dot(last, q[:, MAIN:D])).astype(BF)
            return 0

        lax.fori_loop(0, 3, step, 0)

    for base, count in ((0, 160), (160, 160)):
        pack(base, count)
        each(base // ROWS, (base + count) // ROWS, 0, lambda k: go(k, 0).start())
    stay_go[0].start()
    pack(BASE[1], COUNT[1])

    def gather_last(part):
        base, count = BASE[part], COUNT[part]
        i, j = iota((count, count), 0), iota((count, count), 1)
        total = None
        for t in range(3):
            pick = ones_where((i >> 4 == j >> 4) & ((i & 15) == (j & 15) - CAP + 4 * t) & ((j & 15) >= CAP))
            term = dot(pick, arrived[base : base + count, t * PART : (t + 1) * PART])
            total = term if total is None else total + term
        lastq[base : base + count, :] = total.astype(BF)

    def logits(part, begin, steps, size):
        base, count = BASE[part], COUNT[part]

        def step(j, _):
            rows = pl.ds(pl.multiple_of(lax.rem((begin + j) * size, KEYS), size), size)
            total = dot_t(arrived[base : base + count, 0:MAIN], keys[part, rows, 0:MAIN])
            total = total + dot_t(lastq[base : base + count, :], keys[part, rows, MAIN:D])
            lg[base : base + count, rows] = total * SCALE
            return 0

        lax.fori_loop(0, steps, step, 0)

    def softmax(part):
        base, count = BASE[part], COUNT[part]
        sub = 64
        kblock = iota((128, KEYS), 1) >> 6
        spread = ones_where(kblock == iota((128, KEYS), 0))

        def step(i, _):
            rows = pl.ds(pl.multiple_of(base + i * sub, sub), sub)
            tags = arrived[rows, MAIN:WIDE]
            l = lg[rows, :]
            high = tags[:, 16:17].astype(F32)
            pos = (high * 64.0 + tags[:, 17:18].astype(F32)).astype(jnp.int32)
            key = iota((sub, KEYS), 1)
            allowed = (dot(tags, spread) > 0.5) | (key >> 6 == high.astype(jnp.int32))
            hot = key == pos
            usable = jnp.where(allowed, l, -1e30)
            top = jnp.max(usable, axis=1, keepdims=True)
            e = jnp.exp(usable - top)
            total = jnp.sum(e, axis=1, keepdims=True)
            lse = top + jnp.log(total)
            loss = lse - jnp.sum(jnp.where(hot, l, 0.0), axis=1, keepdims=True)
            probs = (e * (1.0 / total)).astype(BF).astype(F32)
            wts[rows, :] = jnp.where(hot, probs - 1.0, probs).astype(BF)
            back[rows, MAIN:WIDE] = jnp.where(iota((sub, 128), 1) == 0, loss, 0.0).astype(BF)
            return 0

        lax.fori_loop(0, count // sub, step, 0)

    def pull(part, sent):
        base, count = BASE[part], COUNT[part]
        lastg[0:count, :] = (dot(wts[base : base + count, :], keys[part, :, MAIN:D]) * SCALE).astype(BF)
        i, j = iota((count, count), 0), iota((count, count), 1)
        upper = iota((count, 1), 0) & 15

        for t in range(3):
            cols = slice(t * PART, (t + 1) * PART)
            main = dot(wts[base : base + count, :], keys[part, :, cols]) * SCALE
            put = ones_where((i >> 4 == j >> 4) & ((i & 15) >= CAP) & ((j & 15) == (i & 15) - CAP + 4 * t))
            low = dot(put, lastg[0:count, :])
            back[base : base + count, cols] = jnp.where(upper < CAP, main, low).astype(BF)
            sent(t)

    for s, h in ((1, 0), (1, 1), (2, 0), (2, 1), (3, 0), (3, 1)):
        ring_step(0, s, h)
    ring_begin(1)
    ring_step(0, 4, 0)
    ring_step(0, 4, 1)
    for i in range(5):
        sibling_done(0, i)
    get_bank.wait()

    all_go(0).wait_recv()
    stay_go[0].wait()
    each(NA, PIECES, 1, lambda k: go(k, 1).start())
    stay_go[1].start()
    gather_last(0)
    ring_step(1, 1, 0)
    logits(0, 0, KEYS // KTILE, KTILE)
    ring_step(1, 1, 1)
    softmax(0)
    ring_step(1, 2, 0)

    def sent_first(t):
        each(0, NA, 0, lambda k: come(k, 0, t).start())
        if t == 2:
            stay_come[0].start()

    pull(0, sent_first)
    ring_step(1, 2, 1)
    all_go(1).wait_recv()
    stay_go[1].wait()
    gather_last(1)
    ring_step(1, 3, 0)
    ring_step(1, 3, 1)
    eye = iota((QDEV, QDEV), 0) == iota((QDEV, QDEV), 1)
    lane = iota((QDEV, 128), 1)
    for i, row in enumerate((slot.astype(F32), slot_last.astype(F32), third.astype(F32), weight_ref[...])):
        column = jnp.sum(jnp.where(eye, row, 0.0), axis=1, keepdims=True)
        place[...] = jnp.where(lane == i, column, 0.0 if i == 0 else place[...])
    put_place = pltpu.make_async_copy(place, place_hbm, local_sem.at[6])
    put_place.start()
    for i in range(3):
        sibling_done(1, i)
    logits(1, y + NY - 2, 5, 2 * BROWS)
    sibling_done(1, 3)
    logits(1, y + 3, 1, 2 * BROWS)
    logits(1, y + 5, 1, 2 * BROWS)
    ring_end(0)
    ring_step(1, 4, 0)
    ring_step(1, 4, 1)
    sibling_done(1, 4)

    logits(1, y + 4, 1, 2 * BROWS)
    softmax(1)

    def sent_second(t):
        each(NA, PIECES, 1, lambda k: come(k, 1, t).start())
        if t == 2:
            stay_come[1].start()

    pull(1, sent_second)
    ring_end(1)
    z_copy(0).wait_send()
    z_copy(1).wait_send()
    all_go(0).wait_send()
    all_go(1).wait_send()

    put_place.wait()
    stay_come[0].wait()
    stay_come[1].wait()
    for part in (0, 1):
        all_come(part).wait_send()
        all_come(part).wait_recv()


def finish(place_hbm, home_hbm, grad_hbm, loss_ref, place, home, grad, in_sem, out_sem):
    def get(t):
        cols = pl.ds(t * PART, PART) if t < 3 else pl.ds(MAIN, 128)
        return pltpu.make_async_copy(home_hbm.at[:, cols], home.at[:, cols], in_sem.at[t])

    def put(t):
        cols = pl.ds(t * PART, PART)
        return pltpu.make_async_copy(grad.at[:, cols], grad_hbm.at[:, cols], out_sem.at[t])

    get_place = pltpu.make_async_copy(place_hbm, place, in_sem.at[4])
    get_place.start()
    for t in range(4):
        get(t).start()
    get_place.wait()
    slot, slot_last, third = [place[:, i : i + 1].astype(jnp.int32) for i in range(3)]
    weight = place[:, 3:4]
    col = iota((QDEV, PIECES * ROWS), 1)
    main = ones_where(slot == col)
    total = None
    for t in range(3):
        cols = slice(t * PART, (t + 1) * PART)
        get(t).wait()
        both = jnp.concatenate([main, ones_where((slot_last == col) & (third == t))], axis=0)
        moved = dot(both, home[:, cols])
        grad[:, cols] = (moved[:QDEV] * weight).astype(BF)
        put(t).start()
        term = moved[QDEV:]
        total = term if total is None else total + term
    grad[:, MAIN:D] = (total * weight).astype(BF)
    put(3).start()
    get(3).wait()
    losses = dot(main, home[:, MAIN:WIDE])
    eye = iota((QDEV, QDEV), 0) == iota((QDEV, QDEV), 1)
    loss_ref[...] = jnp.sum(jnp.where(eye, losses[:, 0:1], 0.0), axis=0, keepdims=True).reshape(QDEV).astype(BF)
    for t in range(4):
        put(t).wait()


def body(queries, bank, cluster_ids, block_lists, positive_ids, loss_weights):
    vmem = pl.BlockSpec(memory_space=pltpu.VMEM)
    hbm = pl.BlockSpec(memory_space=pl.ANY)
    dma = pltpu.SemaphoreType.DMA
    slots = (PIECES * ROWS, WIDE)
    place, home = pl.pallas_call(
        kernel,
        out_shape=(
            jax.ShapeDtypeStruct((QDEV, 128), F32),
            jax.ShapeDtypeStruct(slots, BF),
        ),
        in_specs=[vmem, vmem, vmem, vmem, hbm, hbm],
        out_specs=(hbm, hbm),
        scratch_shapes=[
            pltpu.VMEM((QDEV, D), BF),
            pltpu.VMEM((2, KEYS, D), BF),
            pltpu.VMEM(slots, BF),
            pltpu.VMEM(slots, BF),
            pltpu.VMEM(slots, BF),
            pltpu.VMEM((PIECES * ROWS, PART), BF),
            pltpu.VMEM((PIECES * ROWS, KEYS), F32),
            pltpu.VMEM((PIECES * ROWS, KEYS), BF),
            pltpu.VMEM((COUNT[0], PART), BF),
            pltpu.VMEM((QDEV, 128), F32),
            dma((7,)),
            dma((2, 2)),
            dma((2,)),
            dma((2,)),
            dma((2,)),
            dma((2,)),
            dma((2, 2, 4, 2)),
            dma((2, 2, 4, 2)),
            dma((2, 2, 5, 2)),
            dma((2, 2, 5, 2)),
        ],
        compiler_params=pltpu.CompilerParams(
            collective_id=0, has_side_effects=True, vmem_limit_bytes=60 * 1024 * 1024
        ),
        cost_estimate=pl.CostEstimate(flops=10**10, bytes_accessed=10**7, transcendentals=10**6),
    )(
        cluster_ids.reshape(1, QDEV),
        block_lists.T,
        positive_ids.reshape(1, QDEV),
        loss_weights.reshape(1, QDEV),
        queries,
        bank,
    )
    grad, loss = pl.pallas_call(
        finish,
        out_shape=(jax.ShapeDtypeStruct((QDEV, D), BF), jax.ShapeDtypeStruct((QDEV,), BF)),
        in_specs=[hbm, hbm],
        out_specs=(hbm, vmem),
        scratch_shapes=[
            pltpu.VMEM((QDEV, 128), F32),
            pltpu.VMEM(slots, BF),
            pltpu.VMEM((QDEV, D), BF),
            dma((5,)),
            dma((4,)),
        ],
        compiler_params=pltpu.CompilerParams(vmem_limit_bytes=60 * 1024 * 1024),
        cost_estimate=pl.CostEstimate(flops=10**9, bytes_accessed=5 * 10**6, transcendentals=0),
    )(place, home)
    return grad, loss


def solution(mesh):
    rows = P(("clu", "bank"), None)
    flat = P(("clu", "bank"))
    return jax.shard_map(
        body,
        mesh=mesh,
        in_specs=(rows, rows, rows, rows, flat, flat),
        out_specs=(rows, flat),
        check_vma=False,
    )
```
